32 devices in a mesh: groups: 2 (over y), layer: 4 (over z), ex: 4 (over x, core).
Axes of the slice: x: 2, y: 2, z: 4, core: 2. Of those that a mesh axis runs over, the one named last changes fastest.
Arguments:
- acts: bfloat16 [4, 8, 256, 4096], P('layer', ('groups', 'ex')), parts along dimension 1, may hold values from -6 to 6
- grads: bfloat16 [4, 8, 256, 1024], P('layer', ('groups', 'ex')), parts along dimension 1, may hold values from -6 to 6
- proj_in: bfloat16 [4, 128, 4096], P('layer'), may hold values from -0.09375 to 0.09375
- proj_out: bfloat16 [4, 128, 1024], P('layer'), may hold values from -0.1875 to 0.1875
- queries: bfloat16 [512, 16384], P('layer', 'ex'), may hold values from -0.046875 to 0.046875
Outputs:
- scores: float32 [8, 512], P(('groups', 'ex'), 'layer'), parts along dimension 0
The draws below stay inside these ranges and needn't reach their ends.
There are 2 independent parts, one for each index of `groups`. The reference program is written for one: setup_inputs(seed, part) draws one part's arguments, and reference() takes and returns one part's arrays. A program takes and returns all parts, laid end to end along the dimension named above; an argument that names none is the same for every part. Nothing has to cross between parts.
All inputs are finite; a program needn't handle non-finite values.
Results may differ from the reference program's by a relative error of at most 0.005.
Values may be sent and summed in bfloat16 or wider, within the bound.
No kernel may reach another device: no remote copies, remote signals or barrier semaphores. Data moves between devices by JAX's collectives and lax.ppermute only.
A program may use at most 64 MiB of HBM per device.

```python
import math
import jax
import jax.numpy as jnp
from jax import lax

DIN = 4096
DOUT = 1024
KI = 128
KO = 128
SEQ = 256
FEAT = 16384
LAYERS = 4
EXAMPLES = 4
NQ = 512


def levels(rng, shape, cuts, low, high):
    loudness, own = 1.0, jax.random.fold_in(rng, 6)
    for dim, blocks in cuts:
        draws = jnp.exp(jax.random.uniform(jax.random.fold_in(own, dim), (blocks,), jnp.float32, low / len(cuts), high / len(cuts)))
        loudness = loudness * jnp.repeat(draws, shape[dim] // blocks).reshape([-1 if axis == dim else 1 for axis in range(len(shape))])
    return loudness


def noise(rng, shape, spread, bound, split=(), kind=jnp.bfloat16):
    loudness = levels(rng, shape, split, -0.22, 0.18) if split else 1.0
    entries = jax.random.normal(rng, shape, jnp.float32) * spread * loudness
    return jnp.minimum(jnp.maximum(entries, -bound), bound).astype(kind)


def setup_inputs(seed: int = 0, part: int = 0) -> dict:
    seeds = jax.random.split(jax.random.key(seed), 6)
    own_keys = jax.random.split(jax.random.fold_in(seeds[5], part), 6)
    return {
        "acts": noise(own_keys[0], (LAYERS, EXAMPLES, SEQ, DIN), 1.0, 6.0, ((0, 4), (1, 4))),
        "grads": noise(own_keys[1], (LAYERS, EXAMPLES, SEQ, DOUT), 1.0, 6.0, ((0, 4), (1, 4))),
        "proj_in": noise(seeds[2], (LAYERS, KI, DIN), DIN ** -0.5, 0.09375, ((0, 4),)),
        "proj_out": noise(seeds[3], (LAYERS, KO, DOUT), DOUT ** -0.5, 0.1875, ((0, 4),)),
        "queries": noise(seeds[4], (NQ, FEAT), FEAT ** -0.5, 0.046875, ((0, 4), (1, 4))),
    }


def reference(acts, grads, proj_in, proj_out, queries):

    def one_layer(total, layer):
        x, g, pin, pout = layer
        x_low = jnp.einsum('esd,bd->esb', x.astype(jnp.float32), pin.astype(jnp.float32)).astype(jnp.bfloat16)
        g_low = jnp.einsum('eso,ao->esa', g.astype(jnp.float32), pout.astype(jnp.float32)).astype(jnp.bfloat16)
        outer = jnp.einsum('esa,esb->eab', g_low.astype(jnp.float32), x_low.astype(jnp.float32))
        return (total + outer.reshape(outer.shape[0], KO * KI), None)
    start = jnp.zeros((EXAMPLES, KO * KI), jnp.float32)
    features, unused = lax.scan(one_layer, start, (acts, grads, proj_in, proj_out))
    feat_low = features.astype(jnp.bfloat16)
    scale = 1.0 / math.sqrt(SEQ * LAYERS)
    return jnp.dot(feat_low, queries.T, preferred_element_type=jnp.float32) * scale
```

```python
import math

import jax
import jax.numpy as jnp
from jax import lax
from jax.experimental import pallas as pl
from jax.experimental.pallas import tpu as pltpu
from jax.sharding import PartitionSpec as P

LANES = 128
PIECES = 4
VMEM_SPEC = pl.BlockSpec(memory_space=pltpu.VMEM)
ANY_SPEC = pl.BlockSpec(memory_space=pl.ANY)


def dot_nt(rows, weight):
    return lax.dot_general(
        rows, weight, (((1,), (1,)), ((), ())), preferred_element_type=jnp.float32
    )


def outer_kernel(acts, grads, proj_in, proj_out, low_ref, full_ref, a_buf, g_buf, pi_buf, po_buf, sems):
    width = acts.shape[1] // PIECES
    grad_copies = [
        pltpu.make_async_copy(proj_out, po_buf, sems.at[0]),
        pltpu.make_async_copy(grads, g_buf, sems.at[1]),
    ]
    act_copies = []
    for k in range(PIECES):
        cols = pl.ds(k * width, width)
        act_copies.append((
            pltpu.make_async_copy(proj_in.at[:, cols], pi_buf.at[:, cols], sems.at[2 + 2 * k]),
            pltpu.make_async_copy(acts.at[:, cols], a_buf.at[:, cols], sems.at[3 + 2 * k]),
        ))
    for copy in grad_copies:
        copy.start()
    for pair in act_copies:
        for copy in pair:
            copy.start()
    for copy in grad_copies:
        copy.wait()
    g_low = dot_nt(po_buf[...], g_buf[...]).astype(jnp.bfloat16)
    x_low = None
    for k, pair in enumerate(act_copies):
        for copy in pair:
            copy.wait()
        cols = slice(k * width, (k + 1) * width)
        part = dot_nt(a_buf[:, cols], pi_buf[:, cols])
        x_low = part if x_low is None else x_low + part
    outer = jnp.dot(g_low, x_low.astype(jnp.bfloat16), preferred_element_type=jnp.float32)
    full_ref[...] = outer
    low_ref[...] = outer.astype(jnp.bfloat16)


def outer_product(acts, grads, proj_in, proj_out):
    k_in, k_out = proj_in.shape[0], proj_out.shape[0]
    return pl.pallas_call(
        outer_kernel,
        out_shape=(
            jax.ShapeDtypeStruct((k_out, k_in), jnp.bfloat16),
            jax.ShapeDtypeStruct((k_out, k_in), jnp.float32),
        ),
        in_specs=[ANY_SPEC] * 4,
        out_specs=(VMEM_SPEC, VMEM_SPEC),
        scratch_shapes=[
            pltpu.VMEM(acts.shape, jnp.bfloat16),
            pltpu.VMEM(grads.shape, jnp.bfloat16),
            pltpu.VMEM(proj_in.shape, jnp.bfloat16),
            pltpu.VMEM(proj_out.shape, jnp.bfloat16),
            pltpu.SemaphoreType.DMA((2 + 2 * PIECES,)),
        ],
        compiler_params=pltpu.CompilerParams(vmem_limit_bytes=16 * 2**20),
    )(acts, grads, proj_in, proj_out)


def spread_kernel(count, own, got, *outs):
    me = lax.axis_index("ex")
    rows = own.shape[0] // count
    for m in range(count):
        block = pl.ds(pl.multiple_of((me ^ m) * rows, rows), rows)
        outs[m][...] = (own[block, :] + got[block, :].astype(jnp.float32)).astype(jnp.bfloat16)


def spread(own, got, count):
    rows = own.shape[0] // count
    return pl.pallas_call(
        lambda *refs: spread_kernel(count, *refs),
        out_shape=[jax.ShapeDtypeStruct((rows, own.shape[1]), jnp.bfloat16)] * count,
        in_specs=[VMEM_SPEC] * 2,
        out_specs=[VMEM_SPEC] * count,
    )(own, got)


def score_kernel(count, queries, *refs):
    feats, outs = refs[:count], refs[count:]
    table = jnp.stack([f[...].astype(jnp.float32) for f in feats], axis=0)
    table = jnp.swapaxes(table, 0, 1)
    table = jnp.concatenate([table[a] for a in range(table.shape[0])], axis=1)
    raw = dot_nt(table.astype(jnp.bfloat16), queries[...])
    for m in range(count):
        outs[m][...] = raw[m:m + 1]


def score(queries, feats):
    count = len(feats)
    return pl.pallas_call(
        lambda *refs: score_kernel(count, *refs),
        out_shape=[jax.ShapeDtypeStruct((1, queries.shape[0]), jnp.float32)] * count,
        in_specs=[VMEM_SPEC] * (count + 1),
        out_specs=[VMEM_SPEC] * count,
        compiler_params=pltpu.CompilerParams(vmem_limit_bytes=16 * 2**20),
    )(queries, *feats)


def swap(value, axis, bit):
    size = lax.axis_size(axis)
    return lax.ppermute(value, axis, [(s, s ^ bit) for s in range(size)])


def on_device(acts, grads, proj_in, proj_out, queries):
    layers, count = lax.axis_size("layer"), lax.axis_size("ex")
    tokens = acts.shape[2]
    low, full = outer_product(acts[0, 0], grads[0, 0], proj_in[0], proj_out[0])
    bit = 1
    while bit * 2 < layers:
        full = full + swap(low, "layer", bit).astype(jnp.float32)
        low = full.astype(jnp.bfloat16)
        bit *= 2
    blocks = spread(full, swap(low, "layer", bit), count)
    order = sorted(range(1, count), reverse=True)
    got = {m: swap(blocks[m], "ex", m) for m in order}
    parts = score(queries, [blocks[0]] + [got[m] for m in range(1, count)])
    back = {m: swap(parts[m], "ex", m) for m in order}
    raw = parts[0]
    for m in range(1, count):
        raw = raw + back[m]
    return raw * (1.0 / math.sqrt(tokens * layers))


def solution(mesh):
    placed = (
        P("layer", ("groups", "ex"), None, None),
        P("layer", ("groups", "ex"), None, None),
        P("layer", None, None),
        P("layer", None, None),
        P("layer", "ex"),
    )
    return jax.shard_map(
        on_device,
        mesh=mesh,
        in_specs=placed,
        out_specs=P(("groups", "ex"), "layer"),
        check_vma=False,
    )
```

```python
import math

import jax
import jax.numpy as jnp
from jax import lax
from jax.experimental import pallas as pl
from jax.experimental.pallas import tpu as pltpu
from jax.sharding import PartitionSpec as P

PIECES = 4
VMEM_SPEC = pl.BlockSpec(memory_space=pltpu.VMEM)
HBM_SPEC = pl.BlockSpec(memory_space=pltpu.HBM)
SMALL = pltpu.CompilerParams(vmem_limit_bytes=4 * 2**20)
LARGE = pltpu.CompilerParams(vmem_limit_bytes=16 * 2**20)


def dot_nt(rows, weight):
    return lax.dot_general(
        rows, weight, (((1,), (1,)), ((), ())), preferred_element_type=jnp.float32
    )


def outer_kernel(acts, grads, proj_in, proj_out, low_ref, full_ref, a_buf, g_buf, pi_buf, po_buf, sems):
    width = acts.shape[1] // PIECES
    grad_copies = [
        pltpu.make_async_copy(proj_out, po_buf, sems.at[0]),
        pltpu.make_async_copy(grads, g_buf, sems.at[1]),
    ]
    act_copies = []
    for k in range(PIECES):
        cols = pl.ds(k * width, width)
        act_copies.append((
            pltpu.make_async_copy(proj_in.at[:, cols], pi_buf.at[:, cols], sems.at[2 + 2 * k]),
            pltpu.make_async_copy(acts.at[:, cols], a_buf.at[:, cols], sems.at[3 + 2 * k]),
        ))
    for copy in grad_copies:
        copy.start()
    for pair in act_copies:
        for copy in pair:
            copy.start()
    for copy in grad_copies:
        copy.wait()
    g_low = dot_nt(po_buf[...], g_buf[...]).astype(jnp.bfloat16)
    x_low = None
    for k, pair in enumerate(act_copies):
        for copy in pair:
            copy.wait()
        cols = slice(k * width, (k + 1) * width)
        part = dot_nt(a_buf[:, cols], pi_buf[:, cols])
        x_low = part if x_low is None else x_low + part
    outer = jnp.dot(g_low, x_low.astype(jnp.bfloat16), preferred_element_type=jnp.float32)
    full_ref[...] = outer
    low_ref[...] = outer.astype(jnp.bfloat16)


def outer_product(acts, grads, proj_in, proj_out):
    k_in, k_out = proj_in.shape[0], proj_out.shape[0]
    args = [pltpu.with_memory_space_constraint(a, pltpu.HBM) for a in (acts, grads, proj_in, proj_out)]
    return pl.pallas_call(
        outer_kernel,
        out_shape=(
            jax.ShapeDtypeStruct((k_out, k_in), jnp.bfloat16),
            jax.ShapeDtypeStruct((k_out, k_in), jnp.float32),
        ),
        in_specs=[HBM_SPEC] * 4,
        out_specs=(VMEM_SPEC, VMEM_SPEC),
        scratch_shapes=[
            pltpu.VMEM(acts.shape, jnp.bfloat16),
            pltpu.VMEM(grads.shape, jnp.bfloat16),
            pltpu.VMEM(proj_in.shape, jnp.bfloat16),
            pltpu.VMEM(proj_out.shape, jnp.bfloat16),
            pltpu.SemaphoreType.DMA((2 + 2 * PIECES,)),
        ],
        compiler_params=LARGE,
    )(*args)


def spread_kernel(count, own, got, *outs):
    place = lax.axis_index("ex") // 2
    rows = own.shape[0] // count
    for k in range(count):
        block = pl.ds(pl.multiple_of((place ^ k) * rows, rows), rows)
        outs[k][...] = (own[block, :] + got[block, :].astype(jnp.float32)).astype(jnp.bfloat16)


def spread(own, got, count):
    rows = own.shape[0] // count
    return pl.pallas_call(
        lambda *refs: spread_kernel(count, *refs),
        out_shape=[jax.ShapeDtypeStruct((rows, own.shape[1]), jnp.bfloat16)] * count,
        in_specs=[VMEM_SPEC] * 2,
        out_specs=[VMEM_SPEC] * count,
        compiler_params=SMALL,
    )(own, got)


def score_kernel(count, own, other, *refs):
    feats, outs = refs[:count], refs[count:]
    core = lax.axis_index("ex") % 2
    rows = feats[0].shape[0] // 2
    raw = None
    for side, queries in ((core, own), (1 - core, other)):
        part = pl.ds(pl.multiple_of(side * rows, rows), rows)
        table = jnp.stack([f[part, :].astype(jnp.float32) for f in feats], axis=0)
        table = jnp.swapaxes(table, 0, 1)
        table = jnp.concatenate([table[a] for a in range(rows)], axis=1)
        product = dot_nt(table.astype(jnp.bfloat16), queries[...])
        raw = product if raw is None else raw + product
    for m in range(count):
        outs[m][...] = raw[m:m + 1]


def score(own, other, feats):
    count = len(feats)
    return pl.pallas_call(
        lambda *refs: score_kernel(count, *refs),
        out_shape=[jax.ShapeDtypeStruct((1, own.shape[0]), jnp.float32)] * count,
        in_specs=[VMEM_SPEC] * (count + 2),
        out_specs=[VMEM_SPEC] * count,
        compiler_params=LARGE,
    )(own, other, *feats)


def swap(value, axis, bits):
    size = lax.axis_size(axis)
    return lax.ppermute(value, axis, [(s, s ^ bits) for s in range(size)])


def doublings(size, start=1):
    bits = []
    while start < size:
        bits.append(start)
        start *= 2
    return bits


def on_device(acts, grads, proj_in, proj_out, queries):
    layers, examples = lax.axis_size("layer"), lax.axis_size("ex")
    tokens = acts.shape[2]
    low, full = outer_product(acts[0, 0], grads[0, 0], proj_in[0], proj_out[0])
    *first, last = doublings(layers)
    for bit in first:
        full = full + swap(low, "layer", bit).astype(jnp.float32)
        low = full.astype(jnp.bfloat16)
    other = swap(queries, "ex", 1)
    blocks = spread(full, swap(low, "layer", last), examples // 2)

    slots = {0: blocks}
    for bit in reversed(doublings(examples, 2)):
        half = bit // 2
        kept = {}
        for m, held in slots.items():
            kept[m] = held[:half]
            kept[m ^ bit ^ 1] = [swap(b, "ex", bit | 1) for b in held[half:]]
        slots = kept
    names = sorted(slots)
    parts = dict(zip(names, score(queries, other, [slots[m][0] for m in names])))
    for bit in reversed(doublings(examples, 2)):
        back = {m ^ bit ^ 1: swap(parts[m], "ex", bit | 1) for m in parts if m & bit}
        parts = {m: parts[m] + back[m] for m in parts if not m & bit}
    return parts[0] * (1.0 / math.sqrt(tokens * layers))


def solution(mesh):
    placed = (
        P("layer", ("groups", "ex"), None, None),
        P("layer", ("groups", "ex"), None, None),
        P("layer", None, None),
        P("layer", None, None),
        P("layer", "ex"),
    )
    return jax.shard_map(
        on_device,
        mesh=mesh,
        in_specs=placed,
        out_specs=P(("groups", "ex"), "layer"),
        check_vma=False,
    )
```

```python
import math

import jax
import jax.numpy as jnp
from jax import lax
from jax.experimental import pallas as pl
from jax.experimental.pallas import tpu as pltpu
from jax.sharding import PartitionSpec as P

VMEM_SPEC = pl.BlockSpec(memory_space=pltpu.VMEM)
SMALL = pltpu.CompilerParams(vmem_limit_bytes=4 * 2**20)
LARGE = pltpu.CompilerParams(vmem_limit_bytes=16 * 2**20)


def dot_nt(rows, weight):
    return lax.dot_general(
        rows, weight, (((1,), (1,)), ((), ())), preferred_element_type=jnp.float32
    )


def outer_kernel(x_low, grads, proj_out, low_ref, full_ref):
    g_low = dot_nt(proj_out[...], grads[...]).astype(jnp.bfloat16)
    outer = jnp.dot(g_low, x_low[...], preferred_element_type=jnp.float32)
    full_ref[...] = outer
    low_ref[...] = outer.astype(jnp.bfloat16)


def outer_product(x_low, grads, proj_out):
    shape = (proj_out.shape[0], x_low.shape[1])
    return pl.pallas_call(
        outer_kernel,
        out_shape=(jax.ShapeDtypeStruct(shape, jnp.bfloat16), jax.ShapeDtypeStruct(shape, jnp.float32)),
        in_specs=[VMEM_SPEC] * 3,
        out_specs=(VMEM_SPEC, VMEM_SPEC),
        compiler_params=SMALL,
        name="outer_product",
    )(x_low, grads, proj_out)


def spread_kernel(count, own, got, *outs):
    place = lax.axis_index("ex") // 2
    rows = own.shape[0] // count
    for k in range(count):
        block = pl.ds(pl.multiple_of((place ^ k) * rows, rows), rows)
        outs[k][...] = (own[block, :] + got[block, :].astype(jnp.float32)).astype(jnp.bfloat16)


def spread(own, got, count):
    rows = own.shape[0] // count
    return pl.pallas_call(
        lambda *refs: spread_kernel(count, *refs),
        out_shape=[jax.ShapeDtypeStruct((rows, own.shape[1]), jnp.bfloat16)] * count,
        in_specs=[VMEM_SPEC] * 2,
        out_specs=[VMEM_SPEC] * count,
        compiler_params=SMALL,
        name="spread",
    )(own, got)


def turn_kernel(own, other, out):
    width = own.shape[1]
    out[:width, :] = own[...].T
    out[width:, :] = other[...].T


def turn(own, other):
    return pl.pallas_call(
        turn_kernel,
        out_shape=jax.ShapeDtypeStruct((2 * own.shape[1], own.shape[0]), own.dtype),
        in_specs=[VMEM_SPEC] * 2,
        out_specs=VMEM_SPEC,
        compiler_params=LARGE,
        name="turn",
    )(own, other)


def score_kernel(count, queries, *refs):
    feats, outs = refs[: 2 * count], refs[2 * count:]
    core = lax.axis_index("ex") % 2
    rows = feats[0].shape[0] // 2
    width = queries.shape[0] // 2
    raw = None
    for side, half in ((core, 0), (1 - core, 1)):
        part = pl.ds(pl.multiple_of(side * rows, rows), rows)
        table = jnp.stack(
            [feats[2 * m][part, :].astype(jnp.float32) + feats[2 * m + 1][part, :].astype(jnp.float32)
             for m in range(count)], axis=0)
        table = jnp.swapaxes(table, 0, 1)
        table = jnp.concatenate([table[a] for a in range(rows)], axis=1)
        product = jnp.dot(
            table.astype(jnp.bfloat16), queries[half * width:(half + 1) * width, :],
            preferred_element_type=jnp.float32)
        raw = product if raw is None else raw + product
    for m in range(count):
        outs[m][...] = raw[m:m + 1]


def score(queries, feats):
    count = len(feats)
    return pl.pallas_call(
        lambda *refs: score_kernel(count, *refs),
        out_shape=[jax.ShapeDtypeStruct((1, queries.shape[1]), jnp.float32)] * count,
        in_specs=[VMEM_SPEC] * (2 * count + 1),
        out_specs=[VMEM_SPEC] * count,
        compiler_params=LARGE,
        name="score",
    )(queries, *[f for pair in feats for f in pair])


def swap(value, layer_bits, ex_bits):
    layers, examples = lax.axis_size("layer"), lax.axis_size("ex")
    pairs = [
        (l * examples + e, (l ^ layer_bits) * examples + (e ^ ex_bits))
        for l in range(layers) for e in range(examples)
    ]
    return lax.ppermute(value, ("layer", "ex"), pairs)


def doublings(size, start=1):
    bits = []
    while start < size:
        bits.append(start)
        start *= 2
    return bits


ORDER = (0, 1, 2)


def on_device(acts, grads, proj_in, proj_out, queries):
    layers, examples = lax.axis_size("layer"), lax.axis_size("ex")
    tokens = acts.shape[2]
    x_low = dot_nt(acts[0, 0], proj_in[0]).astype(jnp.bfloat16)
    low, full = outer_product(x_low, grads[0, 0], proj_out[0])
    joint, *first, last = doublings(layers)
    for bit in first:
        full = full + swap(low, bit, 0).astype(jnp.float32)
        low = full.astype(jnp.bfloat16)
    low, queries = lax.optimization_barrier((low, queries))
    got = swap(low, last, 0)
    other = swap(queries, 0, 1)
    blocks = spread(full, got, examples // 2)

    slots = {0: blocks}
    *outer, inner = reversed(doublings(examples, 2))
    for bit in outer:
        half = bit // 2
        kept = {}
        for m, held in slots.items():
            kept[m] = held[:half]
            kept[m ^ bit ^ 1] = [swap(b, 0, bit | 1) for b in held[half:]]
        slots = kept
    pairs = {}
    for m, (keep, give) in slots.items():
        come = {}
        for step in ORDER:
            if step == 0:
                come[0] = swap(give, 0, inner | 1)
            elif step == 1:
                come[1] = swap(keep, joint, 0)
            else:
                come[2] = swap(give, joint, inner | 1)
        pairs[m] = (keep, come[1])
        pairs[m ^ inner ^ 1] = (come[0], come[2])
    names = sorted(pairs)
    table = turn(queries, other)
    parts = dict(zip(names, score(table, [pairs[m] for m in names])))
    for bit in reversed(doublings(examples, 2)):
        back = {m ^ bit ^ 1: swap(parts[m], 0, bit | 1) for m in parts if m & bit}
        parts = {m: parts[m] + back[m] for m in parts if not m & bit}
    return parts[0] * (1.0 / math.sqrt(tokens * layers))


def solution(mesh):
    placed = (
        P("layer", ("groups", "ex"), None, None),
        P("layer", ("groups", "ex"), None, None),
        P("layer", None, None),
        P("layer", None, None),
        P("layer", "ex"),
    )
    return jax.shard_map(
        on_device,
        mesh=mesh,
        in_specs=placed,
        out_specs=P(("groups", "ex"), "layer"),
        check_vma=False,
    )
```

```python
import math

import jax
import jax.numpy as jnp
from jax import lax
from jax.experimental import pallas as pl
from jax.experimental.pallas import tpu as pltpu
from jax.sharding import PartitionSpec as P

PIECES = 2
VMEM_SPEC = pl.BlockSpec(memory_space=pltpu.VMEM)
HBM_SPEC = pl.BlockSpec(memory_space=pltpu.HBM)
SMALL = pltpu.CompilerParams(vmem_limit_bytes=4 * 2**20)
LARGE = pltpu.CompilerParams(vmem_limit_bytes=16 * 2**20)


def dot_nt(rows, weight):
    return lax.dot_general(
        rows, weight, (((1,), (1,)), ((), ())), preferred_element_type=jnp.float32
    )


def outer_kernel(acts, grads, proj_in, proj_out, low_ref, full_ref, a_buf, g_buf, pi_buf, po_buf, sems):
    width = acts.shape[1] // PIECES

    def piece(k):
        cols = pl.ds(k * width if isinstance(k, int) else pl.multiple_of(k * width, width), width)
        return cols, (
            pltpu.make_async_copy(proj_in.at[:, cols], pi_buf.at[:, cols], sems.at[2 + 2 * k]),
            pltpu.make_async_copy(acts.at[:, cols], a_buf.at[:, cols], sems.at[3 + 2 * k]),
        )

    out_copies = (
        pltpu.make_async_copy(proj_out, po_buf, sems.at[0]),
        pltpu.make_async_copy(grads, g_buf, sems.at[1]),
    )
    for copy in out_copies:
        copy.start()
    for k in range(PIECES):
        for copy in piece(k)[1]:
            copy.start()
    for copy in out_copies:
        copy.wait()
    g_low = dot_nt(po_buf[...], g_buf[...]).astype(jnp.bfloat16)

    def add_piece(k, total):
        cols, copies = piece(k)
        for copy in copies:
            copy.wait()
        return total + dot_nt(a_buf[:, cols], pi_buf[:, cols])

    x_low = lax.fori_loop(
        0, PIECES, add_piece, jnp.zeros((acts.shape[0], proj_in.shape[0]), jnp.float32))
    outer = jnp.dot(g_low, x_low.astype(jnp.bfloat16), preferred_element_type=jnp.float32)
    full_ref[...] = outer
    low_ref[...] = outer.astype(jnp.bfloat16)


def outer_product(*args):
    acts, grads, proj_in, proj_out = args
    shape = (proj_out.shape[0], proj_in.shape[0])
    return pl.pallas_call(
        outer_kernel,
        out_shape=(jax.ShapeDtypeStruct(shape, jnp.bfloat16), jax.ShapeDtypeStruct(shape, jnp.float32)),
        in_specs=[HBM_SPEC] * 4,
        out_specs=(VMEM_SPEC, VMEM_SPEC),
        scratch_shapes=[pltpu.VMEM(a.shape, a.dtype) for a in args]
        + [pltpu.SemaphoreType.DMA((2 + 2 * PIECES,))],
        compiler_params=LARGE,
        name="outer_product",
    )(*[pltpu.with_memory_space_constraint(a, pltpu.HBM) for a in args])


def spread_kernel(count, own, got, *outs):
    place = lax.axis_index("ex") // 2
    rows = own.shape[0] // count
    for k in range(count):
        block = pl.ds(pl.multiple_of((place ^ k) * rows, rows), rows)
        total = (own[block, :] + got[block, :].astype(jnp.float32)).astype(jnp.bfloat16)
        outs[k][...] = total
        outs[k + count][...] = total


def spread(own, got, count):
    rows = own.shape[0] // count
    outs = pl.pallas_call(
        lambda *refs: spread_kernel(count, *refs),
        out_shape=[jax.ShapeDtypeStruct((rows, own.shape[1]), jnp.bfloat16)] * (2 * count),
        in_specs=[VMEM_SPEC] * 2,
        out_specs=[VMEM_SPEC] * (2 * count),
        compiler_params=SMALL,
        name="spread",
    )(own, got)
    return list(zip(outs[:count], outs[count:]))


def turn_kernel(own, other, out):
    width = own.shape[1]
    out[:width, :] = own[...].T
    out[width:, :] = other[...].T


def turn(own, other):
    return pl.pallas_call(
        turn_kernel,
        out_shape=jax.ShapeDtypeStruct((2 * own.shape[1], own.shape[0]), own.dtype),
        in_specs=[VMEM_SPEC] * 2,
        out_specs=VMEM_SPEC,
        compiler_params=LARGE,
        name="turn",
    )(own, other)


def score_kernel(count, queries, *refs):
    near, far, outs = refs[:count], refs[count:2 * count], refs[2 * count:]
    core = lax.axis_index("ex") % 2
    rows = near[0].shape[0] // 2
    width = queries.shape[0] // 2
    raw = None
    for side, half in ((core, 0), (1 - core, 1)):
        part = pl.ds(pl.multiple_of(side * rows, rows), rows)
        table = jnp.stack(
            [a[part, :].astype(jnp.float32) + b[part, :].astype(jnp.float32) for a, b in zip(near, far)], axis=0)
        table = jnp.swapaxes(table, 0, 1)
        table = jnp.concatenate([table[a] for a in range(rows)], axis=1)
        product = jnp.dot(
            table.astype(jnp.bfloat16), queries[half * width:(half + 1) * width, :],
            preferred_element_type=jnp.float32)
        raw = product if raw is None else raw + product
    for m in range(count):
        outs[m][...] = raw[m:m + 1]


def score(queries, near, far):
    count = len(near)

    def kernel(queries, *refs):
        half = count // 2
        parts = [refs[k * half:(k + 1) * half] for k in range(4)]
        score_kernel(count, queries, *parts[0], *parts[3], *parts[2], *parts[1], *refs[2 * count:])

    half = count // 2
    return pl.pallas_call(
        kernel,
        out_shape=[jax.ShapeDtypeStruct((1, queries.shape[1]), jnp.float32)] * count,
        in_specs=[VMEM_SPEC] * (2 * count + 1),
        out_specs=[VMEM_SPEC] * count,
        compiler_params=LARGE,
        name="score",
    )(queries, *near[:half], *far[half:], *far[:half], *near[half:])


def swap(value, layer_bits, ex_bits):
    layers, examples = lax.axis_size("layer"), lax.axis_size("ex")
    pairs = [
        (l * examples + e, (l ^ layer_bits) * examples + (e ^ ex_bits))
        for l in range(layers) for e in range(examples)
    ]
    return lax.ppermute(value, ("layer", "ex"), pairs)


def doublings(size, start=1):
    bits = []
    while start < size:
        bits.append(start)
        start *= 2
    return bits


def on_device(acts, grads, proj_in, proj_out, queries):
    layers, examples = lax.axis_size("layer"), lax.axis_size("ex")
    tokens = acts.shape[2]
    other = swap(queries, 0, 1)
    low, full = outer_product(acts[0, 0], grads[0, 0], proj_in[0], proj_out[0])
    joint, *first, last = doublings(layers)
    for bit in first:
        full = full + swap(low, bit, 0).astype(jnp.float32)
        low = full.astype(jnp.bfloat16)
    blocks = spread(full, swap(low, last, 0), examples // 2)

    slots = {0: blocks}
    *outer, inner = reversed(doublings(examples, 2))
    for bit in outer:
        half = bit // 2
        kept = {}
        for m, held in slots.items():
            kept[m] = held[:half]
            kept[m ^ bit ^ 1] = [(come, come) for come in (swap(b, 0, bit | 1) for b, _ in held[half:])]
        slots = kept
    near, far = {}, {}
    for m, ((keep, keep_too), (give, give_too)) in slots.items():
        near[m], far[m] = keep, swap(keep_too, joint, 0)
        near[m ^ inner ^ 1], far[m ^ inner ^ 1] = swap(give, 0, inner | 1), swap(give_too, joint, inner | 1)
    names = list(slots) + [m ^ inner ^ 1 for m in slots]
    scores = score(turn(queries, other), [near[m] for m in names], [far[m] for m in names])
    parts = dict(zip(names, scores))
    for bit in reversed(doublings(examples, 2)):
        back = {m ^ bit ^ 1: swap(parts[m], 0, bit | 1) for m in parts if m & bit}
        parts = {m: parts[m] + back[m] for m in parts if not m & bit}
    return parts[0] * (1.0 / math.sqrt(tokens * layers))


def solution(mesh):
    placed = (
        P("layer", ("groups", "ex"), None, None),
        P("layer", ("groups", "ex"), None, None),
        P("layer", None, None),
        P("layer", None, None),
        P("layer", "ex"),
    )
    return jax.shard_map(
        on_device,
        mesh=mesh,
        in_specs=placed,
        out_specs=P(("groups", "ex"), "layer"),
        check_vma=False,
    )
```

```python
import math

import jax
import jax.numpy as jnp
from jax import lax
from jax.experimental import pallas as pl
from jax.experimental.pallas import tpu as pltpu
from jax.sharding import PartitionSpec as P

PIECES = 2
VMEM_SPEC = pl.BlockSpec(memory_space=pltpu.VMEM)
HBM_SPEC = pl.BlockSpec(memory_space=pltpu.HBM)
SMALL = pltpu.CompilerParams(vmem_limit_bytes=4 * 2**20)
LARGE = pltpu.CompilerParams(vmem_limit_bytes=16 * 2**20)


def dot_nt(rows, weight):
    return lax.dot_general(
        rows, weight, (((1,), (1,)), ((), ())), preferred_element_type=jnp.float32
    )


def outer_kernel(acts, grads, proj_in, proj_out, low_ref, full_ref, a_buf, g_buf, pi_buf, po_buf, sems):
    width = acts.shape[1] // PIECES

    def piece(k):
        cols = pl.ds(k * width if isinstance(k, int) else pl.multiple_of(k * width, width), width)
        return cols, (
            pltpu.make_async_copy(proj_in.at[:, cols], pi_buf.at[:, cols], sems.at[2 + 2 * k]),
            pltpu.make_async_copy(acts.at[:, cols], a_buf.at[:, cols], sems.at[3 + 2 * k]),
        )

    out_copies = (
        pltpu.make_async_copy(proj_out, po_buf, sems.at[0]),
        pltpu.make_async_copy(grads, g_buf, sems.at[1]),
    )
    for copy in out_copies:
        copy.start()
    for k in range(PIECES):
        for copy in piece(k)[1]:
            copy.start()
    for copy in out_copies:
        copy.wait()
    g_low = dot_nt(po_buf[...], g_buf[...]).astype(jnp.bfloat16)

    def add_piece(k, total):
        cols, copies = piece(k)
        for copy in copies:
            copy.wait()
        return total + dot_nt(a_buf[:, cols], pi_buf[:, cols])

    x_low = lax.fori_loop(
        0, PIECES, add_piece, jnp.zeros((acts.shape[0], proj_in.shape[0]), jnp.float32))
    outer = jnp.dot(g_low, x_low.astype(jnp.bfloat16), preferred_element_type=jnp.float32)
    full_ref[...] = outer
    low_ref[...] = outer.astype(jnp.bfloat16)


def outer_product(*args):
    acts, grads, proj_in, proj_out = args
    shape = (proj_out.shape[0], proj_in.shape[0])
    return pl.pallas_call(
        outer_kernel,
        out_shape=(jax.ShapeDtypeStruct(shape, jnp.bfloat16), jax.ShapeDtypeStruct(shape, jnp.float32)),
        in_specs=[HBM_SPEC] * 4,
        out_specs=(VMEM_SPEC, VMEM_SPEC),
        scratch_shapes=[pltpu.VMEM(a.shape, a.dtype) for a in args]
        + [pltpu.SemaphoreType.DMA((2 + 2 * PIECES,))],
        compiler_params=LARGE,
        name="outer_product",
    )(*[pltpu.with_memory_space_constraint(a, pltpu.HBM) for a in args])


def spread_kernel(count, own, got, *outs):
    place = lax.axis_index("ex") // 2
    rows = own.shape[0] // count
    for k in range(count):
        block = pl.ds(pl.multiple_of((place ^ k) * rows, rows), rows)
        total = (own[block, :] + got[block, :].astype(jnp.float32)).astype(jnp.bfloat16)
        outs[k][...] = total
        outs[k + count][...] = total


def spread(own, got, count):
    rows = own.shape[0] // count
    outs = pl.pallas_call(
        lambda *refs: spread_kernel(count, *refs),
        out_shape=[jax.ShapeDtypeStruct((rows, own.shape[1]), jnp.bfloat16)] * (2 * count),
        in_specs=[VMEM_SPEC] * 2,
        out_specs=[VMEM_SPEC] * (2 * count),
        compiler_params=SMALL,
        name="spread",
    )(own, got)
    return list(zip(outs[:count], outs[count:]))


def turn_kernel(own, other, out):
    width = own.shape[1]
    out[:width, :] = own[...].T
    out[width:, :] = other[...].T


def turn(own, other):
    return pl.pallas_call(
        turn_kernel,
        out_shape=jax.ShapeDtypeStruct((2 * own.shape[1], own.shape[0]), own.dtype),
        in_specs=[VMEM_SPEC] * 2,
        out_specs=VMEM_SPEC,
        compiler_params=LARGE,
        name="turn",
    )(own, other)


def score_kernel(count, queries, *refs):
    near, far, outs = refs[:count], refs[count:2 * count], refs[2 * count:]
    core = lax.axis_index("ex") % 2
    rows = near[0].shape[0] // 2
    width = queries.shape[0] // 2
    raw = None
    for side, half in ((core, 0), (1 - core, 1)):
        part = pl.ds(pl.multiple_of(side * rows, rows), rows)
        table = jnp.stack(
            [a[part, :].astype(jnp.float32) + b[part, :].astype(jnp.float32) for a, b in zip(near, far)], axis=0)
        table = jnp.swapaxes(table, 0, 1)
        table = jnp.concatenate([table[a] for a in range(rows)], axis=1)
        product = jnp.dot(
            table.astype(jnp.bfloat16), queries[half * width:(half + 1) * width, :],
            preferred_element_type=jnp.float32)
        raw = product if raw is None else raw + product
    for m in range(count):
        outs[m][...] = raw[m:m + 1]


def score(queries, near, far):
    count = len(near)
    return pl.pallas_call(
        lambda *refs: score_kernel(count, *refs),
        out_shape=[jax.ShapeDtypeStruct((1, queries.shape[1]), jnp.float32)] * count,
        in_specs=[VMEM_SPEC] * (2 * count + 1),
        out_specs=[VMEM_SPEC] * count,
        compiler_params=LARGE,
        name="score",
    )(queries, *near, *far)


def swap(value, layer_bits, ex_bits):
    layers, examples = lax.axis_size("layer"), lax.axis_size("ex")
    pairs = [
        (l * examples + e, (l ^ layer_bits) * examples + (e ^ ex_bits))
        for l in range(layers) for e in range(examples)
    ]
    return lax.ppermute(value, ("layer", "ex"), pairs)


def cross(value, early, layer_bits, ex_bits):
    layers, examples = lax.axis_size("layer"), lax.axis_size("ex")
    pairs = [
        (l * examples + e, (l ^ layer_bits if (e % 4 == 2) == early else l) * examples + (e ^ ex_bits))
        for l in range(layers) for e in range(examples)
    ]
    return lax.ppermute(value, ("layer", "ex"), pairs)


def doublings(size, start=1):
    bits = []
    while start < size:
        bits.append(start)
        start *= 2
    return bits


def on_device(acts, grads, proj_in, proj_out, queries):
    layers, examples = lax.axis_size("layer"), lax.axis_size("ex")
    tokens = acts.shape[2]
    other = swap(queries, 0, 1)
    low, full = outer_product(acts[0, 0], grads[0, 0], proj_in[0], proj_out[0])
    joint, *first, last = doublings(layers)
    for bit in first:
        full = full + swap(low, bit, 0).astype(jnp.float32)
        low = full.astype(jnp.bfloat16)
    blocks = spread(full, swap(low, last, 0), examples // 2)

    slots = {0: blocks}
    *outer, inner = reversed(doublings(examples, 2))
    for bit in outer:
        half = bit // 2
        kept = {}
        for m, held in slots.items():
            kept[m] = held[:half]
            kept[m ^ bit ^ 1] = [(come, come) for come in (swap(b, 0, bit | 1) for b, _ in held[half:])]
        slots = kept
    near, far = {}, {}
    for m, ((keep, keep_too), (give, give_too)) in slots.items():
        near[m], far[m] = keep, swap(keep_too, joint, 0)
        near[m ^ inner ^ 1], far[m ^ inner ^ 1] = cross(give, False, joint, inner | 1), cross(give_too, True, joint, inner | 1)
    names = list(slots) + [m ^ inner ^ 1 for m in slots]
    table = turn(queries, other)
    away = [m for m in names if m]
    parts = dict(zip(away, score(table, [far[m] for m in away], [near[m] for m in away])))
    (parts[0],) = score(table, [far[0]], [near[0]])
    for bit in reversed(doublings(examples, 2)):
        back = {m ^ bit ^ 1: swap(parts[m], 0, bit | 1) for m in parts if m & bit}
        parts = {m: parts[m] + back[m] for m in parts if not m & bit}
    return parts[0] * (1.0 / math.sqrt(tokens * layers))


def solution(mesh):
    placed = (
        P("layer", ("groups", "ex"), None, None),
        P("layer", ("groups", "ex"), None, None),
        P("layer", None, None),
        P("layer", None, None),
        P("layer", "ex"),
    )
    return jax.shard_map(
        on_device,
        mesh=mesh,
        in_specs=placed,
        out_specs=P(("groups", "ex"), "layer"),
        check_vma=False,
    )
```

```python
import math

import jax
import jax.numpy as jnp
from jax import lax
from jax.experimental import pallas as pl
from jax.experimental.pallas import tpu as pltpu
from jax.sharding import PartitionSpec as P

PIECES = 2
VMEM_SPEC = pl.BlockSpec(memory_space=pltpu.VMEM)
HBM_SPEC = pl.BlockSpec(memory_space=pltpu.HBM)
SMALL = pltpu.CompilerParams(vmem_limit_bytes=4 * 2**20)
LARGE = pltpu.CompilerParams(vmem_limit_bytes=16 * 2**20)


def dot_nt(rows, weight):
    return lax.dot_general(
        rows, weight, (((1,), (1,)), ((), ())), preferred_element_type=jnp.float32
    )


def outer_kernel(count, acts, grads, proj_in, proj_out, low_own, low_rest, full_own, full_rest,
                 total, a_buf, g_buf, pi_buf, po_buf, sems):
    width = acts.shape[1] // PIECES

    def piece(k):
        cols = pl.ds(k * width if isinstance(k, int) else pl.multiple_of(k * width, width), width)
        return cols, (
            pltpu.make_async_copy(proj_in.at[:, cols], pi_buf.at[:, cols], sems.at[2 + 2 * k]),
            pltpu.make_async_copy(acts.at[:, cols], a_buf.at[:, cols], sems.at[3 + 2 * k]),
        )

    out_copies = (
        pltpu.make_async_copy(proj_out, po_buf, sems.at[0]),
        pltpu.make_async_copy(grads, g_buf, sems.at[1]),
    )
    for copy in out_copies:
        copy.start()
    for k in range(PIECES):
        for copy in piece(k)[1]:
            copy.start()
    for copy in out_copies:
        copy.wait()
    g_low = dot_nt(po_buf[...], g_buf[...]).astype(jnp.bfloat16)

    def add_piece(k, total):
        cols, copies = piece(k)
        for copy in copies:
            copy.wait()
        return total + dot_nt(a_buf[:, cols], pi_buf[:, cols])

    x_low = lax.fori_loop(
        0, PIECES, add_piece, jnp.zeros((acts.shape[0], proj_in.shape[0]), jnp.float32))
    outer = jnp.dot(g_low, x_low.astype(jnp.bfloat16), preferred_element_type=jnp.float32)
    total[...] = outer
    place = lax.axis_index("ex") // 2
    rows = total.shape[0] // count
    for k in range(count):
        block = total[pl.ds(pl.multiple_of((place ^ k) * rows, rows), rows), :]
        if k == 0:
            full_own[...] = block
            low_own[...] = block.astype(jnp.bfloat16)
        else:
            full_rest[(k - 1) * rows:k * rows, :] = block
            low_rest[(k - 1) * rows:k * rows, :] = block.astype(jnp.bfloat16)


def outer_product(count, *args):
    acts, grads, proj_in, proj_out = args
    rows, width = proj_out.shape[0] // count, proj_in.shape[0]
    rest = rows * (count - 1)
    return pl.pallas_call(
        lambda *refs: outer_kernel(count, *refs),
        out_shape=[jax.ShapeDtypeStruct((n, width), t) for t in (jnp.bfloat16, jnp.float32) for n in (rows, rest)],
        in_specs=[HBM_SPEC] * 4,
        out_specs=[VMEM_SPEC] * 4,
        scratch_shapes=[pltpu.VMEM((rows * count, width), jnp.float32)]
        + [pltpu.VMEM(a.shape, a.dtype) for a in args]
        + [pltpu.SemaphoreType.DMA((2 + 2 * PIECES,))],
        compiler_params=LARGE,
        name="outer_product",
    )(*[pltpu.with_memory_space_constraint(a, pltpu.HBM) for a in args])


def spread_kernel(count, own, got, *outs):
    rows = own.shape[0] // count
    for k in range(count):
        block = slice(k * rows, (k + 1) * rows)
        total = (own[block, :] + got[block, :].astype(jnp.float32)).astype(jnp.bfloat16)
        outs[k][...] = total
        outs[k + count][...] = total


def spread(own, got, count):
    rows = own.shape[0] // count
    outs = pl.pallas_call(
        lambda *refs: spread_kernel(count, *refs),
        out_shape=[jax.ShapeDtypeStruct((rows, own.shape[1]), jnp.bfloat16)] * (2 * count),
        in_specs=[VMEM_SPEC] * 2,
        out_specs=[VMEM_SPEC] * (2 * count),
        compiler_params=SMALL,
        name="spread",
    )(own, got)
    return list(zip(outs[:count], outs[count:]))


def turn_kernel(own, other, out):
    width = own.shape[1]
    out[:width, :] = own[...].T
    out[width:, :] = other[...].T


def turn(own, other):
    return pl.pallas_call(
        turn_kernel,
        out_shape=jax.ShapeDtypeStruct((2 * own.shape[1], own.shape[0]), own.dtype),
        in_specs=[VMEM_SPEC] * 2,
        out_specs=VMEM_SPEC,
        compiler_params=LARGE,
        name="turn",
    )(own, other)


def score_kernel(count, queries, *refs):
    near, far, outs = refs[:count], refs[count:2 * count], refs[2 * count:]
    core = lax.axis_index("ex") % 2
    rows = near[0].shape[0] // 2
    width = queries.shape[0] // 2
    raw = None
    for side, half in ((core, 0), (1 - core, 1)):
        part = pl.ds(pl.multiple_of(side * rows, rows), rows)
        table = jnp.stack(
            [a[part, :].astype(jnp.float32) + b[part, :].astype(jnp.float32) for a, b in zip(near, far)], axis=0)
        table = jnp.swapaxes(table, 0, 1)
        table = jnp.concatenate([table[a] for a in range(rows)], axis=1)
        product = jnp.dot(
            table.astype(jnp.bfloat16), queries[half * width:(half + 1) * width, :],
            preferred_element_type=jnp.float32)
        raw = product if raw is None else raw + product
    for m in range(count):
        outs[m][...] = raw[m:m + 1]


def score(queries, near, far):
    count = len(near)
    return pl.pallas_call(
        lambda *refs: score_kernel(count, *refs),
        out_shape=[jax.ShapeDtypeStruct((1, queries.shape[1]), jnp.float32)] * count,
        in_specs=[VMEM_SPEC] * (2 * count + 1),
        out_specs=[VMEM_SPEC] * count,
        compiler_params=LARGE,
        name="score",
    )(queries, *near, *far)


def swap(value, layer_bits, ex_bits):
    layers, examples = lax.axis_size("layer"), lax.axis_size("ex")
    pairs = [
        (l * examples + e, (l ^ layer_bits) * examples + (e ^ ex_bits))
        for l in range(layers) for e in range(examples)
    ]
    return lax.ppermute(value, ("layer", "ex"), pairs)


def cross(value, early, layer_bits, ex_bits):
    layers, examples = lax.axis_size("layer"), lax.axis_size("ex")
    pairs = [
        (l * examples + e, (l ^ layer_bits if (e % 4 == 2) == early else l) * examples + (e ^ ex_bits))
        for l in range(layers) for e in range(examples)
    ]
    return lax.ppermute(value, ("layer", "ex"), pairs)


def doublings(size, start=1):
    bits = []
    while start < size:
        bits.append(start)
        start *= 2
    return bits


def on_device(acts, grads, proj_in, proj_out, queries):
    layers, examples = lax.axis_size("layer"), lax.axis_size("ex")
    tokens = acts.shape[2]
    other = swap(queries, 0, 1)
    count = examples // 2
    *low, full_own, full_rest = outer_product(count, acts[0, 0], grads[0, 0], proj_in[0], proj_out[0])
    full = [full_own, full_rest]
    joint, *first, last = doublings(layers)
    for bit in first:
        full = [f + swap(a, bit, 0).astype(jnp.float32) for a, f in zip(low, full)]
        low = [f.astype(jnp.bfloat16) for f in full]
    got, table = lax.optimization_barrier((swap(low[1], last, 0), turn(queries, other)))
    rest = spread(full[1], got, count - 1)
    blocks = spread(full[0], swap(low[0], last, 0), 1) + rest

    slots = {0: blocks}
    *outer, inner = reversed(doublings(examples, 2))
    for bit in outer:
        half = bit // 2
        kept = {}
        for m, held in slots.items():
            kept[m] = held[:half]
            kept[m ^ bit ^ 1] = [(come, come) for come in (swap(b, 0, bit | 1) for b, _ in held[half:])]
        slots = kept
    near, far = {}, {}
    for m, ((keep, keep_too), (give, give_too)) in slots.items():
        near[m], far[m] = keep, swap(keep_too, joint, 0)
        near[m ^ inner ^ 1], far[m ^ inner ^ 1] = cross(give, False, joint, inner | 1), cross(give_too, True, joint, inner | 1)
    names = list(slots) + [m ^ inner ^ 1 for m in slots]
    away = [m for m in names if m]
    parts = dict(zip(away, score(table, [far[m] for m in away], [near[m] for m in away])))
    (parts[0],) = score(table, [far[0]], [near[0]])
    for bit in reversed(doublings(examples, 2)):
        back = {m ^ bit ^ 1: swap(parts[m], 0, bit | 1) for m in parts if m & bit}
        parts = {m: parts[m] + back[m] for m in parts if not m & bit}
    return parts[0] * (1.0 / math.sqrt(tokens * layers))


def solution(mesh):
    placed = (
        P("layer", ("groups", "ex"), None, None),
        P("layer", ("groups", "ex"), None, None),
        P("layer", None, None),
        P("layer", None, None),
        P("layer", "ex"),
    )
    return jax.shard_map(
        on_device,
        mesh=mesh,
        in_specs=placed,
        out_specs=P(("groups", "ex"), "layer"),
        check_vma=False,
    )
```

```python
import math

import jax
import jax.numpy as jnp
from jax import lax
from jax.experimental import pallas as pl
from jax.experimental.pallas import tpu as pltpu
from jax.sharding import PartitionSpec as P

PIECES = 2
VMEM_SPEC = pl.BlockSpec(memory_space=pltpu.VMEM)
HBM_SPEC = pl.BlockSpec(memory_space=pltpu.HBM)
SMALL = pltpu.CompilerParams(vmem_limit_bytes=4 * 2**20)
LARGE = pltpu.CompilerParams(vmem_limit_bytes=16 * 2**20)


def dot_nt(rows, weight):
    return lax.dot_general(
        rows, weight, (((1,), (1,)), ((), ())), preferred_element_type=jnp.float32
    )


def outer_kernel(count, acts, grads, proj_in, proj_out, low_own, low_rest, full_own, full_rest,
                 total, a_buf, g_buf, pi_buf, po_buf, sems):
    width = acts.shape[1] // PIECES

    def piece(k):
        cols = pl.ds(k * width if isinstance(k, int) else pl.multiple_of(k * width, width), width)
        return cols, (
            pltpu.make_async_copy(acts.at[:, cols], a_buf.at[:, cols], sems.at[3 + 2 * k]),
            pltpu.make_async_copy(proj_in.at[:, cols], pi_buf.at[:, cols], sems.at[2 + 2 * k]),
        )

    out_copies = (
        pltpu.make_async_copy(proj_out, po_buf, sems.at[0]),
        pltpu.make_async_copy(grads, g_buf, sems.at[1]),
    )
    for copy in out_copies:
        copy.start()
    for k in range(PIECES):
        for copy in piece(k)[1]:
            copy.start()
    for copy in out_copies:
        copy.wait()
    g_low = dot_nt(po_buf[...], g_buf[...]).astype(jnp.bfloat16)

    def add_piece(k, total):
        cols, copies = piece(k)
        for copy in copies:
            copy.wait()
        return total + dot_nt(a_buf[:, cols], pi_buf[:, cols])

    x_low = lax.fori_loop(
        0, PIECES, add_piece, jnp.zeros((acts.shape[0], proj_in.shape[0]), jnp.float32))
    outer = jnp.dot(g_low, x_low.astype(jnp.bfloat16), preferred_element_type=jnp.float32)
    total[...] = outer
    place = lax.axis_index("ex") // 2
    rows = total.shape[0] // count
    for k in range(count):
        block = total[pl.ds(pl.multiple_of((place ^ k) * rows, rows), rows), :]
        if k == 0:
            full_own[...] = block
            low_own[...] = block.astype(jnp.bfloat16)
        else:
            full_rest[(k - 1) * rows:k * rows, :] = block
            low_rest[(k - 1) * rows:k * rows, :] = block.astype(jnp.bfloat16)


def outer_product(count, *args):
    acts, grads, proj_in, proj_out = args
    rows, width = proj_out.shape[0] // count, proj_in.shape[0]
    rest = rows * (count - 1)
    return pl.pallas_call(
        lambda *refs: outer_kernel(count, *refs),
        out_shape=[jax.ShapeDtypeStruct((n, width), t) for t in (jnp.bfloat16, jnp.float32) for n in (rows, rest)],
        in_specs=[HBM_SPEC] * 4,
        out_specs=[VMEM_SPEC] * 4,
        scratch_shapes=[pltpu.VMEM((rows * count, width), jnp.float32)]
        + [pltpu.VMEM(a.shape, a.dtype) for a in args]
        + [pltpu.SemaphoreType.DMA((2 + 2 * PIECES,))],
        compiler_params=LARGE,
        name="outer_product",
    )(*[pltpu.with_memory_space_constraint(a, pltpu.HBM) for a in args])


def spread_kernel(count, own, got, *outs):
    rows = own.shape[0] // count
    for k in range(count):
        block = slice(k * rows, (k + 1) * rows)
        total = (own[block, :] + got[block, :].astype(jnp.float32)).astype(jnp.bfloat16)
        outs[k][...] = total
        outs[k + count][...] = total


def spread(own, got, count):
    rows = own.shape[0] // count
    outs = pl.pallas_call(
        lambda *refs: spread_kernel(count, *refs),
        out_shape=[jax.ShapeDtypeStruct((rows, own.shape[1]), jnp.bfloat16)] * (2 * count),
        in_specs=[VMEM_SPEC] * 2,
        out_specs=[VMEM_SPEC] * (2 * count),
        compiler_params=SMALL,
        name="spread",
    )(own, got)
    return list(zip(outs[:count], outs[count:]))


def turn_kernel(own, other, out):
    width = own.shape[1]
    out[:width, :] = own[...].T
    out[width:, :] = other[...].T


def turn(own, other):
    return pl.pallas_call(
        turn_kernel,
        out_shape=jax.ShapeDtypeStruct((2 * own.shape[1], own.shape[0]), own.dtype),
        in_specs=[VMEM_SPEC] * 2,
        out_specs=VMEM_SPEC,
        compiler_params=LARGE,
        name="turn",
    )(own, other)


def score_kernel(count, queries, *refs):
    near, far, outs = refs[:count], refs[count:2 * count], refs[2 * count:]
    core = lax.axis_index("ex") % 2
    rows = near[0].shape[0] // 2
    width = queries.shape[0] // 2
    raw = None
    for side, half in ((core, 0), (1 - core, 1)):
        part = pl.ds(pl.multiple_of(side * rows, rows), rows)
        table = jnp.stack(
            [a[part, :].astype(jnp.float32) + b[part, :].astype(jnp.float32) for a, b in zip(near, far)], axis=0)
        table = jnp.swapaxes(table, 0, 1)
        table = jnp.concatenate([table[a] for a in range(rows)], axis=1)
        product = jnp.dot(
            table.astype(jnp.bfloat16), queries[half * width:(half + 1) * width, :],
            preferred_element_type=jnp.float32)
        raw = product if raw is None else raw + product
    for m in range(count):
        outs[m][...] = raw[m:m + 1]


def score(queries, near, far):
    count = len(near)
    return pl.pallas_call(
        lambda *refs: score_kernel(count, *refs),
        out_shape=[jax.ShapeDtypeStruct((1, queries.shape[1]), jnp.float32)] * count,
        in_specs=[VMEM_SPEC] * (2 * count + 1),
        out_specs=[VMEM_SPEC] * count,
        compiler_params=LARGE,
        name="score",
    )(queries, *near, *far)


def swap(value, layer_bits, ex_bits):
    layers, examples = lax.axis_size("layer"), lax.axis_size("ex")
    pairs = [
        (l * examples + e, (l ^ layer_bits) * examples + (e ^ ex_bits))
        for l in range(layers) for e in range(examples)
    ]
    return lax.ppermute(value, ("layer", "ex"), pairs)


def cross(value, early, layer_bits, ex_bits):
    layers, examples = lax.axis_size("layer"), lax.axis_size("ex")
    pairs = [
        (l * examples + e, (l ^ layer_bits if (e % 4 == 2) == early else l) * examples + (e ^ ex_bits))
        for l in range(layers) for e in range(examples)
    ]
    return lax.ppermute(value, ("layer", "ex"), pairs)


def doublings(size, start=1):
    bits = []
    while start < size:
        bits.append(start)
        start *= 2
    return bits


def on_device(acts, grads, proj_in, proj_out, queries):
    layers, examples = lax.axis_size("layer"), lax.axis_size("ex")
    tokens = acts.shape[2]
    other = swap(queries, 0, 1)
    count = examples // 2
    *low, full_own, full_rest = outer_product(count, acts[0, 0], grads[0, 0], proj_in[0], proj_out[0])
    full = [full_own, full_rest]
    joint, *first, last = doublings(layers)
    for bit in first:
        full = [f + swap(a, bit, 0).astype(jnp.float32) for a, f in zip(low, full)]
        low = [f.astype(jnp.bfloat16) for f in full]
    got, table = lax.optimization_barrier((swap(low[1], last, 0), turn(queries, other)))
    rest = spread(full[1], got, count - 1)
    blocks = spread(full[0], swap(low[0], last, 0), 1) + rest

    slots = {0: blocks}
    *outer, inner = reversed(doublings(examples, 2))
    for bit in outer:
        half = bit // 2
        kept = {}
        for m, held in slots.items():
            kept[m] = held[:half]
            kept[m ^ bit ^ 1] = [(come, come) for come in (swap(b, 0, bit | 1) for b, _ in held[half:])]
        slots = kept
    near, far = {}, {}
    for m, ((keep, keep_too), (give, give_too)) in slots.items():
        near[m], far[m] = keep, swap(keep_too, joint, 0)
        near[m ^ inner ^ 1], far[m ^ inner ^ 1] = cross(give, False, joint, inner | 1), cross(give_too, True, joint, inner | 1)
    names = list(slots) + [m ^ inner ^ 1 for m in slots]
    away = [m for m in names if m]
    parts = dict(zip(away, score(table, [far[m] for m in away], [near[m] for m in away])))
    (parts[0],) = score(table, [far[0]], [near[0]])
    for bit in reversed(doublings(examples, 2)):
        back = {m ^ bit ^ 1: swap(parts[m], 0, bit | 1) for m in parts if m & bit}
        parts = {m: parts[m] + back[m] for m in parts if not m & bit}
    return parts[0] * (1.0 / math.sqrt(tokens * layers))


def solution(mesh):
    placed = (
        P("layer", ("groups", "ex"), None, None),
        P("layer", ("groups", "ex"), None, None),
        P("layer", None, None),
        P("layer", None, None),
        P("layer", "ex"),
    )
    return jax.shard_map(
        on_device,
        mesh=mesh,
        in_specs=placed,
        out_specs=P(("groups", "ex"), "layer"),
        check_vma=False,
    )
```

```python
import math

import jax
import jax.numpy as jnp
from jax import lax
from jax.experimental import pallas as pl
from jax.experimental.pallas import tpu as pltpu
from jax.sharding import PartitionSpec as P

PIECES = 2
VMEM_SPEC = pl.BlockSpec(memory_space=pltpu.VMEM)
HBM_SPEC = pl.BlockSpec(memory_space=pltpu.HBM)
SMALL = pltpu.CompilerParams(vmem_limit_bytes=4 * 2**20)
LARGE = pltpu.CompilerParams(vmem_limit_bytes=16 * 2**20)


def dot_nt(rows, weight):
    return lax.dot_general(
        rows, weight, (((1,), (1,)), ((), ())), preferred_element_type=jnp.float32
    )


def outer_kernel(count, acts, grads, proj_in, proj_out, low_own, low_rest, full_own, full_rest,
                 total, a_buf, g_buf, pi_buf, po_buf, sems):
    width = acts.shape[1] // PIECES

    def piece(k):
        cols = pl.ds(k * width if isinstance(k, int) else pl.multiple_of(k * width, width), width)
        return cols, (
            pltpu.make_async_copy(acts.at[:, cols], a_buf.at[:, cols], sems.at[3 + 2 * k]),
            pltpu.make_async_copy(proj_in.at[:, cols], pi_buf.at[:, cols], sems.at[2 + 2 * k]),
        )

    out_copies = (
        pltpu.make_async_copy(proj_out, po_buf, sems.at[0]),
        pltpu.make_async_copy(grads, g_buf, sems.at[1]),
    )
    for copy in out_copies:
        copy.start()
    for k in range(PIECES):
        for copy in piece(k)[1]:
            copy.start()
    for copy in out_copies:
        copy.wait()
    g_low = dot_nt(po_buf[...], g_buf[...]).astype(jnp.bfloat16)

    def add_piece(k, total):
        cols, copies = piece(k)
        for copy in copies:
            copy.wait()
        return total + dot_nt(a_buf[:, cols], pi_buf[:, cols])

    x_low = lax.fori_loop(
        0, PIECES, add_piece, jnp.zeros((acts.shape[0], proj_in.shape[0]), jnp.float32))
    outer = jnp.dot(g_low, x_low.astype(jnp.bfloat16), preferred_element_type=jnp.float32)
    total[...] = outer
    place = lax.axis_index("ex") // 2
    rows = total.shape[0] // count
    for k in range(count):
        block = total[pl.ds(pl.multiple_of((place ^ k) * rows, rows), rows), :]
        if k == 0:
            full_own[...] = block
            low_own[...] = block.astype(jnp.bfloat16)
        else:
            full_rest[(k - 1) * rows:k * rows, :] = block
            low_rest[(k - 1) * rows:k * rows, :] = block.astype(jnp.bfloat16)


def outer_product(count, *args):
    acts, grads, proj_in, proj_out = args
    rows, width = proj_out.shape[0] // count, proj_in.shape[0]
    rest = rows * (count - 1)
    return pl.pallas_call(
        lambda *refs: outer_kernel(count, *refs),
        out_shape=[jax.ShapeDtypeStruct((n, width), t) for t in (jnp.bfloat16, jnp.float32) for n in (rows, rest)],
        in_specs=[HBM_SPEC] * 4,
        out_specs=[VMEM_SPEC] * 4,
        scratch_shapes=[pltpu.VMEM((rows * count, width), jnp.float32)]
        + [pltpu.VMEM(a.shape, a.dtype) for a in args]
        + [pltpu.SemaphoreType.DMA((2 + 2 * PIECES,))],
        compiler_params=LARGE,
        name="outer_product",
    )(*[pltpu.with_memory_space_constraint(a, pltpu.HBM) for a in args])


def spread_kernel(count, own, got, *outs):
    rows = own.shape[0] // count
    for k in range(count):
        block = slice(k * rows, (k + 1) * rows)
        total = (own[block, :] + got[block, :].astype(jnp.float32)).astype(jnp.bfloat16)
        outs[k][...] = total
        outs[k + count][...] = total


def spread(own, got, count):
    rows = own.shape[0] // count
    outs = pl.pallas_call(
        lambda *refs: spread_kernel(count, *refs),
        out_shape=[jax.ShapeDtypeStruct((rows, own.shape[1]), jnp.bfloat16)] * (2 * count),
        in_specs=[VMEM_SPEC] * 2,
        out_specs=[VMEM_SPEC] * (2 * count),
        compiler_params=SMALL,
        name="spread",
    )(own, got)
    return list(zip(outs[:count], outs[count:]))


def turn_kernel(own, other, out):
    width = own.shape[1]
    out[:width, :] = own[...].T
    out[width:, :] = other[...].T


def turn(own, other):
    return pl.pallas_call(
        turn_kernel,
        out_shape=jax.ShapeDtypeStruct((2 * own.shape[1], own.shape[0]), own.dtype),
        in_specs=[VMEM_SPEC] * 2,
        out_specs=VMEM_SPEC,
        compiler_params=LARGE,
        name="turn",
    )(own, other)


def score_kernel(count, queries, *refs):
    near, far, outs = refs[:count], refs[count:2 * count], refs[2 * count:]
    core = lax.axis_index("ex") % 2
    rows = near[0].shape[0] // 2
    width = queries.shape[0] // 2
    raw = None
    for side, half in ((core, 0), (1 - core, 1)):
        part = pl.ds(pl.multiple_of(side * rows, rows), rows)
        table = jnp.stack(
            [a[part, :].astype(jnp.float32) + b[part, :].astype(jnp.float32) for a, b in zip(near, far)], axis=0)
        table = jnp.swapaxes(table, 0, 1)
        table = jnp.concatenate([table[a] for a in range(rows)], axis=1)
        product = jnp.dot(
            table.astype(jnp.bfloat16), queries[half * width:(half + 1) * width, :],
            preferred_element_type=jnp.float32)
        raw = product if raw is None else raw + product
    for m in range(count):
        outs[m][...] = raw[m:m + 1]


def score(queries, near, far):
    count = len(near)
    return pl.pallas_call(
        lambda *refs: score_kernel(count, *refs),
        out_shape=[jax.ShapeDtypeStruct((1, queries.shape[1]), jnp.float32)] * count,
        in_specs=[VMEM_SPEC] * (2 * count + 1),
        out_specs=[VMEM_SPEC] * count,
        compiler_params=LARGE,
        name="score",
    )(queries, *near, *far)


def swap(value, layer_bits, ex_bits):
    layers, examples = lax.axis_size("layer"), lax.axis_size("ex")
    pairs = [
        (l * examples + e, (l ^ layer_bits) * examples + (e ^ ex_bits))
        for l in range(layers) for e in range(examples)
    ]
    return lax.ppermute(value, ("layer", "ex"), pairs)


def cross(value, early, layer_bits, ex_bits):
    layers, examples = lax.axis_size("layer"), lax.axis_size("ex")
    pairs = [
        (l * examples + e, (l ^ layer_bits if (e % 4 == 2) == early else l) * examples + (e ^ ex_bits))
        for l in range(layers) for e in range(examples)
    ]
    return lax.ppermute(value, ("layer", "ex"), pairs)


def doublings(size, start=1):
    bits = []
    while start < size:
        bits.append(start)
        start *= 2
    return bits


def on_device(acts, grads, proj_in, proj_out, queries):
    layers, examples = lax.axis_size("layer"), lax.axis_size("ex")
    tokens = acts.shape[2]
    other = swap(queries, 0, 1)
    count = examples // 2
    *low, full_own, full_rest = outer_product(count, acts[0, 0], grads[0, 0], proj_in[0], proj_out[0])
    full = [full_own, full_rest]
    low[1], late_queries = lax.optimization_barrier((low[1], queries))
    joint, *first, last = doublings(layers)
    for bit in first:
        full = [f + swap(a, bit, 0).astype(jnp.float32) for a, f in zip(low, full)]
        low = [f.astype(jnp.bfloat16) for f in full]
    got, table = lax.optimization_barrier((swap(low[1], last, 0), turn(late_queries, other)))
    rest = spread(full[1], got, count - 1)
    blocks = spread(full[0], swap(low[0], last, 0), 1) + rest

    slots = {0: blocks}
    *outer, inner = reversed(doublings(examples, 2))
    for bit in outer:
        half = bit // 2
        kept = {}
        for m, held in slots.items():
            kept[m] = held[:half]
            kept[m ^ bit ^ 1] = [(come, come) for come in (swap(b, 0, bit | 1) for b, _ in held[half:])]
        slots = kept
    near, far = {}, {}
    for m, ((keep, keep_too), (give, give_too)) in slots.items():
        near[m], far[m] = keep, swap(keep_too, joint, 0)
        near[m ^ inner ^ 1], far[m ^ inner ^ 1] = cross(give, False, joint, inner | 1), cross(give_too, True, joint, inner | 1)
    names = list(slots) + [m ^ inner ^ 1 for m in slots]
    away = [m for m in names if m]
    parts = dict(zip(away, score(table, [far[m] for m in away], [near[m] for m in away])))
    (parts[0],) = score(table, [far[0]], [near[0]])
    for bit in reversed(doublings(examples, 2)):
        back = {m ^ bit ^ 1: swap(parts[m], 0, bit | 1) for m in parts if m & bit}
        parts = {m: parts[m] + back[m] for m in parts if not m & bit}
    return parts[0] * (1.0 / math.sqrt(tokens * layers))


def solution(mesh):
    placed = (
        P("layer", ("groups", "ex"), None, None),
        P("layer", ("groups", "ex"), None, None),
        P("layer", None, None),
        P("layer", None, None),
        P("layer", "ex"),
    )
    return jax.shard_map(
        on_device,
        mesh=mesh,
        in_specs=placed,
        out_specs=P(("groups", "ex"), "layer"),
        check_vma=False,
    )
```
